256 devices in a mesh: row: 16 (over z, core), col: 16 (over x, y).
Axes of the slice: x: 4, y: 4, z: 8, core: 2. Of those that a mesh axis runs over, the one named last changes fastest.
Arguments:
- kernel: bfloat16 [4096, 16, 128, 128], P('row', 'col'), may hold values from -110 to 130
- tile_cols: int32 [4096, 16], P('row', 'col'), may hold values from 0 to 4095, as said below
- start_pot: float32 [524288], P('col'), may hold values from -452 to 2
- log_source: float32 [524288], P('row'), may hold values from -1 to 1
- log_target: float32 [524288], P('col'), may hold values from -1 to 1
- dustbin: float32 [524288], P('col'), may hold values from -1 to 2
Outputs:
- source_pot: float32 [524288], P('row')
- target_pot: float32 [524288], P('col')
The draws below stay inside these ranges and needn't reach their ends.
Inputs may be any that keep to these rules, and one draw needn't show every extreme that they name: `tile_cols`: the 16 slots of one source tile name distinct column tiles. Among the tiles held by one device (one index of row and of col), at most 48 name column tiles of any one col block, and in each row block one col block is named by exactly 48 tiles of every device.
All inputs are finite; a program needn't handle non-finite values.
Results may differ from the reference program's by a relative error of at most 0.0003.
Values sent between devices are 32-bit elements; how exact they have to be, the bound alone decides.
No kernel may reach another device: no remote copies, remote signals or barrier semaphores. Data moves between devices by JAX's collectives and lax.ppermute only.
A program may use at most 64 MiB of HBM per device.

```python
import jax
import jax.numpy as jnp
from jax import lax

TILE = 128
K = 16
ITERS = 2
RTB = 256
CTB = 256
RT = 4096
CT = 4096
NS = 524288
NT = 524288
CAP = 48
N_ROW = 16
N_COL = 16


def draw_kernel(key, part):
    key = jax.random.fold_in(key, 13)
    key_level, key_noise = jax.random.split(key, 2)
    level_index = (jax.random.permutation(key_level, RT * K) % 4).reshape(RT * K)
    level_table = jnp.array([-100.0, 0.0, 50.0, 120.0], jnp.float32)
    level = jnp.sum(level_table[None, :] * (level_index[:, None] == jnp.arange(4)[None, :]).astype(jnp.float32), axis=1)
    level = level.reshape(RT, K)
    noise = jnp.clip(1.5 * jax.random.normal(key_noise, (RT, K, TILE, TILE), jnp.float32), -9.0, 9.0)
    return (noise + level[:, :, None, None]).astype(jnp.bfloat16)


def draw_tile_cols(key, part):
    key = jax.random.fold_in(key, 7)
    key_hot, key_perm, key_start = jax.random.split(key, 3)
    local_slots = K // N_COL
    per_device = RTB * local_slots
    hot_block = jax.random.randint(key_hot, (N_ROW,), 0, N_COL)
    base_count = (per_device - CAP) // (N_COL - 1)
    remainder = (per_device - CAP) % (N_COL - 1)
    blocks = jnp.arange(N_COL)
    ranking = (blocks[None, :] - hot_block[:, None] - 1) % N_COL
    counts = jnp.where(ranking == N_COL - 1, CAP, base_count + (ranking < remainder).astype(jnp.int32))
    ends = jnp.cumsum(counts, axis=1)
    position = jnp.arange(per_device)
    sorted_owner = jnp.sum((position[None, :, None] >= ends[:, None, :]).astype(jnp.int32), axis=2)
    perm_keys = jax.random.split(key_perm, N_ROW * N_COL)
    perms = jax.vmap(lambda one_key: jax.random.permutation(one_key, per_device))(perm_keys)
    perms = perms.reshape(N_ROW, N_COL, per_device)
    owner = jnp.take_along_axis(jnp.broadcast_to(sorted_owner[:, None, :], (N_ROW, N_COL, per_device)), perms, axis=2)
    owner = owner.reshape(N_ROW, N_COL, RTB, local_slots).transpose(0, 2, 1, 3)
    start_tile = jax.random.randint(key_start, (N_ROW, RTB, 1, 1), 0, CTB)
    slot_number = (jnp.arange(N_COL)[:, None] * local_slots + jnp.arange(local_slots)[None, :])[None, None, :, :]
    local_tile = (start_tile + slot_number) % CTB
    return (owner * CTB + local_tile).reshape(N_ROW * RTB, K).astype(jnp.int32)


def draw_start_pot(key, part):
    key = jax.random.fold_in(key, 11)
    return jax.random.uniform(key, (NT,), jnp.float32, -2.0, 2.0)


def block_scale(stream_key, dims, cuts, smallest, high):
    def one(axis_at, shards_of):
        steps = jax.random.uniform(jax.random.fold_in(jax.random.fold_in(stream_key, 6), axis_at), (shards_of,), jnp.float32, smallest / len(cuts), high / len(cuts))
        return jnp.repeat(jnp.exp(steps), dims[axis_at] // shards_of).reshape((-1,) + (1,) * (len(dims) - axis_at - 1))

    gain = one(*cuts[0])
    for cut in cuts[1:]:
        gain = gain * one(*cut)
    return gain


def setup_inputs(seed: int = 0) -> dict:
    seeds = jax.random.split(jax.random.key(seed), 7)
    kernel = draw_kernel(jax.random.fold_in(seeds[6], 71), 0)
    tile_cols = draw_tile_cols(jax.random.fold_in(seeds[6], 71), 0)
    start_pot = draw_start_pot(jax.random.fold_in(seeds[6], 71), 0)
    log_source = jnp.clip(jax.random.uniform(seeds[3], (NS,), jnp.float32, -1.0, 1.0) * block_scale(seeds[3], (NS,), ((0, 16),), -0.4, 0.0), -1.0, 1.0)
    log_target = jnp.clip(jax.random.uniform(seeds[4], (NT,), jnp.float32, -1.0, 1.0) * block_scale(seeds[4], (NT,), ((0, 16),), -0.4, 0.0), -1.0, 1.0)
    dustbin = jnp.clip(-1.0 + 3.0 * jax.random.uniform(seeds[5], (NT,), jnp.float32) ** block_scale(seeds[5], (NT,), ((0, 16),), -0.2, 0.2), -1.0, 2.0)
    return dict(kernel=kernel, tile_cols=tile_cols, start_pot=start_pot, log_source=log_source, log_target=log_target, dustbin=dustbin)


NEGATIVE = -1.0e30


def reference(kernel, tile_cols, start_pot, log_source, log_target, dustbin):
    blocks = kernel.reshape(N_ROW, RTB, K, TILE, TILE)
    slot_cols = tile_cols.reshape(N_ROW, RTB, K)
    flat_cols = tile_cols.reshape(RT * K)
    target_now = start_pot.reshape(CT, TILE)
    source_rows = log_source.reshape(RT, TILE)
    target_rows = log_target.reshape(CT, TILE)
    dust_rows = dustbin.reshape(CT, TILE)
    source_now = source_rows
    for repeat in range(ITERS):
        def row_block(pair):
            tiles, named = pair
            scores = tiles.astype(jnp.float32) + target_now[named][:, :, None, :]
            highest = jnp.max(scores, axis=(1, 3))
            summed = jnp.sum(jnp.exp(scores - highest[:, None, :, None]), axis=(1, 3))
            return highest + jnp.log(summed)

        row_lse = lax.map(row_block, (blocks, slot_cols)).reshape(RT, TILE)
        source_now = source_rows - row_lse
        source_view = source_now.reshape(N_ROW, RTB, TILE)

        def col_block(pair):
            tiles, potential = pair
            scores = tiles.astype(jnp.float32) + potential[:, None, :, None]
            highest = jnp.max(scores, axis=2)
            summed = jnp.sum(jnp.exp(scores - highest[:, :, None, :]), axis=2)
            return highest, summed

        col_high, col_sum = lax.map(col_block, (blocks, source_view))
        col_high = col_high.reshape(RT * K, TILE)
        col_sum = col_sum.reshape(RT * K, TILE)
        seg_high = jnp.maximum(jax.ops.segment_max(col_high, flat_cols, num_segments=CT), NEGATIVE)
        seg_sum = jax.ops.segment_sum(col_sum * jnp.exp(col_high - seg_high[flat_cols]), flat_cols, num_segments=CT)
        top_value = jnp.maximum(seg_high, dust_rows)
        col_lse = top_value + jnp.log(seg_sum * jnp.exp(seg_high - top_value) + jnp.exp(dust_rows - top_value))
        target_now = target_rows - col_lse
    return source_now.reshape(NS), target_now.reshape(NT)
```

```python
import functools

import jax
import jax.numpy as jnp
from jax import lax
from jax.experimental import pallas as pl
from jax.experimental.pallas import tpu as pltpu
from jax.sharding import PartitionSpec as P

ITERS = 2
NEGATIVE = -1e30
VMEM = pltpu.VMEM
SMEM = pltpu.SMEM
VMEM_BYTES = 24 << 20
UNROLL = 16


def spec(space):
    return pl.BlockSpec(memory_space=space)


def params():
    return pltpu.CompilerParams(vmem_limit_bytes=VMEM_BYTES)


def plan_kernel(block_tiles, capacity, cols_ref, slot_ref, ask_ref, count_ref):
    tile_count = slot_ref.shape[0]
    asked = ask_ref.shape[0]

    def clear(step, carry):
        for k in range(16):
            ask_ref[step * 16 + k] = block_tiles
        return carry

    lax.fori_loop(0, asked // 16, clear, 0)
    for k in range(count_ref.shape[0]):
        count_ref[k] = 0

    def place(step, carry):
        for k in range(8):
            n = step * 8 + k
            column = cols_ref[n]
            owner = column // block_tiles
            rank = count_ref[owner]
            count_ref[owner] = rank + 1
            slot = owner * capacity + rank
            slot_ref[n] = slot
            ask_ref[slot] = column - owner * block_tiles
        return carry

    lax.fori_loop(0, tile_count // 8, place, 0)


def plan(cols, block_tiles, capacity, owners):
    return pl.pallas_call(
        functools.partial(plan_kernel, block_tiles, capacity),
        name="plan",
        out_shape=(
            jax.ShapeDtypeStruct(cols.shape, jnp.int32),
            jax.ShapeDtypeStruct((owners * capacity,), jnp.int32),
        ),
        in_specs=[spec(SMEM)],
        out_specs=(spec(SMEM), spec(SMEM)),
        scratch_shapes=[SMEM((owners,), jnp.int32)],
    )(cols)


def pick_kernel(ids_ref, rows_ref, out_ref):
    last = rows_ref.shape[0] - 1

    def step(p, carry):
        for k in range(16):
            n = p * 16 + k
            out_ref[pl.ds(n, 1), :] = rows_ref[pl.ds(jnp.minimum(ids_ref[n], last), 1), :]
        return carry

    lax.fori_loop(0, out_ref.shape[0] // 16, step, 0)


def pick(ids, rows):
    return pl.pallas_call(
        pick_kernel,
        name="pick",
        out_shape=jax.ShapeDtypeStruct((ids.shape[0], rows.shape[1]), jnp.float32),
        in_specs=[spec(SMEM), spec(VMEM)],
        out_specs=spec(VMEM),
        compiler_params=params(),
    )(ids, rows)


def row_kernel(slot_ref, tiles_ref, pots_ref, out_ref):
    def step(g, carry):
        tops, sums = [], []
        for k in range(UNROLL):
            n = g * UNROLL + k
            pot = pots_ref[pl.ds(slot_ref[n], 1), :]
            scores = jnp.transpose(tiles_ref[n].astype(jnp.float32) + pot)
            top = jnp.max(scores, axis=0, keepdims=True)
            tops.append(top)
            sums.append(jnp.sum(jnp.exp(scores - top), axis=0, keepdims=True))
        block = pl.ds(pl.multiple_of(g * UNROLL, UNROLL), UNROLL)
        out_ref[block, :] = jnp.concatenate(tops, 0) + jnp.log(jnp.concatenate(sums, 0))
        return carry

    lax.fori_loop(0, tiles_ref.shape[0] // UNROLL, step, 0)


def row_pass(slot, tiles, pots):
    return pl.pallas_call(
        row_kernel,
        name="row_pass",
        out_shape=jax.ShapeDtypeStruct(tiles.shape[:2], jnp.float32),
        in_specs=[spec(SMEM), spec(VMEM), spec(VMEM)],
        out_specs=spec(VMEM),
        compiler_params=params(),
    )(slot, tiles, pots)


def col_kernel(slot_ref, tiles_ref, pots_ref, out_ref, row_ref):
    out_ref[...] = jnp.full(out_ref.shape, NEGATIVE, jnp.float32)
    width = tiles_ref.shape[1]

    def step(g, carry):
        tops, sums = [], []
        for k in range(UNROLL):
            n = g * UNROLL + k
            pot = jnp.broadcast_to(pots_ref[pl.ds(n, 1), :], (width, width))
            scores = tiles_ref[n].astype(jnp.float32) + jnp.transpose(pot)
            top = jnp.max(scores, axis=0, keepdims=True)
            tops.append(top)
            sums.append(jnp.sum(jnp.exp(scores - top), axis=0, keepdims=True))
        row_ref[...] = jnp.concatenate(tops, 0) + jnp.log(jnp.concatenate(sums, 0))
        for k in range(UNROLL):
            out_ref[pl.ds(slot_ref[g * UNROLL + k], 1), :] = row_ref[pl.ds(k, 1), :]
        return carry

    lax.fori_loop(0, tiles_ref.shape[0] // UNROLL, step, 0)


def col_pass(slot, tiles, pots, slots):
    width = tiles.shape[1]
    return pl.pallas_call(
        col_kernel,
        name="col_pass",
        out_shape=jax.ShapeDtypeStruct((slots, width), jnp.float32),
        in_specs=[spec(SMEM), spec(VMEM), spec(VMEM)],
        out_specs=spec(VMEM),
        scratch_shapes=[VMEM((UNROLL, width), jnp.float32)],
        compiler_params=params(),
    )(slot, tiles, pots)


def segment_kernel(ids_ref, rows_ref, out_ref, top_ref, *parts):
    groups = len(parts)
    each = rows_ref.shape[0] // groups
    for part in parts:
        part[...] = jnp.full(part.shape, NEGATIVE, jnp.float32)

    def highest(p, carry):
        for k in range(4):
            for g, part in enumerate(parts):
                n = g * each + p * 4 + k
                here = pl.ds(ids_ref[n], 1)
                part[here, :] = jnp.maximum(part[here, :], rows_ref[pl.ds(n, 1), :])
        return carry

    lax.fori_loop(0, each // 4, highest, 0)
    top = parts[0][...]
    for part in parts[1:]:
        top = jnp.maximum(top, part[...])
    top_ref[...] = top
    for part in parts:
        part[...] = jnp.zeros(part.shape, jnp.float32)

    def add(p, carry):
        for k in range(4):
            for g, part in enumerate(parts):
                n = g * each + p * 4 + k
                here = pl.ds(ids_ref[n], 1)
                part[here, :] = part[here, :] + jnp.exp(rows_ref[pl.ds(n, 1), :] - top_ref[here, :])
        return carry

    lax.fori_loop(0, each // 4, add, 0)
    total = parts[0][...]
    for part in parts[1:]:
        total = total + part[...]
    count = out_ref.shape[0]
    total = total[:count]
    some = total > 0.0
    out_ref[...] = jnp.where(
        some, top_ref[:count, :] + jnp.log(jnp.where(some, total, 1.0)), NEGATIVE
    )


def segment(ids, rows, count):
    width = rows.shape[1]
    return pl.pallas_call(
        segment_kernel,
        name="segment",
        out_shape=jax.ShapeDtypeStruct((count, width), jnp.float32),
        in_specs=[spec(SMEM), spec(VMEM)],
        out_specs=spec(VMEM),
        scratch_shapes=[VMEM((count + 8, width), jnp.float32)] * 9,
        compiler_params=params(),
    )(ids, rows)


def exchange(value, owners):
    shape = value.shape
    return lax.all_to_all(
        value.reshape((owners, shape[0] // owners) + shape[1:]),
        "col",
        split_axis=0,
        concat_axis=0,
        tiled=True,
    ).reshape(shape)


def log_add(a, b):
    return jnp.maximum(a, b) + jnp.log(1.0 + jnp.exp(-jnp.abs(a - b)))


def swap(value, axis, partner):
    return lax.ppermute(value, axis, [(i, j) for i, j in enumerate(partner)])


def col_partners(count):
    return [
        [i ^ 1 for i in range(count)],
        [i ^ 3 for i in range(count)],
        [i ^ 4 for i in range(count)],
        [i ^ 12 for i in range(count)],
    ]


def row_partners(count):
    steps = ([1, 0, 3, 2, 5, 4, 7, 6], [7, 2, 1, 4, 3, 6, 5, 0], [3, 6, 5, 0, 7, 2, 1, 4])
    return [[2 * z[i // 2] + i % 2 for i in range(count)] for z in steps]


def body(kernel, tile_cols, start_pot, log_source, log_target, dustbin):
    row_tiles, local_slots, width, _ = kernel.shape
    owners = lax.axis_size("col")
    block_tiles = start_pot.shape[0] // width
    tile_count = row_tiles * local_slots
    capacity = min(tile_count // 2, 3 * tile_count // owners)
    slots = owners * capacity
    half = block_tiles // 2
    core = lax.axis_index("row") % 2
    other_core = [i ^ 1 for i in range(lax.axis_size("row"))]

    tiles = kernel.reshape(tile_count, width, width)
    target_now = start_pot.reshape(block_tiles, width)
    source_rows = log_source.reshape(row_tiles, width)

    def mine(value, side):
        return lax.dynamic_slice_in_dim(value, side * half, half, 0)

    target_half = mine(log_target.reshape(block_tiles, width), core)
    dust_half = mine(dustbin.reshape(block_tiles, width), core)

    slot, ask = plan(tile_cols.reshape(tile_count), block_tiles, capacity, owners)
    ids = exchange(ask, owners)
    for repeat in range(ITERS):
        pots = exchange(pick(ids, target_now), owners)
        row_lse = row_pass(slot, tiles, pots)
        for partner in col_partners(owners):
            row_lse = log_add(row_lse, swap(row_lse, "col", partner))
        source_now = source_rows - row_lse
        rows = exchange(col_pass(slot, tiles, source_now, slots), owners)
        part = segment(ids, rows, block_tiles)
        col_lse = log_add(mine(part, core), swap(mine(part, 1 - core), "row", other_core))
        for partner in row_partners(len(other_core)):
            col_lse = log_add(col_lse, swap(col_lse, "row", partner))
        here = target_half - log_add(col_lse, dust_half)
        there = swap(here, "row", other_core)
        target_now = jnp.where(
            core == 0, jnp.concatenate([here, there]), jnp.concatenate([there, here])
        )
    return source_now.reshape(log_source.shape), target_now.reshape(start_pot.shape)


def solution(mesh):
    placed = (P("row", "col", None, None), P("row", "col"), P("col"), P("row"), P("col"), P("col"))
    return jax.shard_map(
        body, mesh=mesh, in_specs=placed, out_specs=(P("row"), P("col")), check_vma=False
    )
```

```python
import functools

import jax
import jax.numpy as jnp
from jax import lax
from jax.experimental import pallas as pl
from jax.experimental.pallas import tpu as pltpu
from jax.sharding import PartitionSpec as P

ITERS = 2
NEGATIVE = -1e30
VMEM = pltpu.VMEM
SMEM = pltpu.SMEM
VMEM_BYTES = 48 << 20
CHUNKS = 4
UNROLL = 64
EXTRA = 8


def spec(space):
    return pl.BlockSpec(memory_space=space)


def params():
    return pltpu.CompilerParams(vmem_limit_bytes=VMEM_BYTES)


def plan(cols, block_tiles, owners, width):
    owner = cols // block_tiles
    local = cols % block_tiles
    order = jnp.arange(cols.shape[0])
    before = (owner[:, None] == owner[None, :]) & (order[None, :] < order[:, None])
    rank = jnp.sum(before.astype(jnp.int32), axis=1)
    lane = (owner * width + rank)[:, None] == jnp.arange(owners * width)[None, :]
    ask = block_tiles + jnp.sum(jnp.where(lane, local[:, None] - block_tiles, 0), axis=0)
    return owner, local, rank, ask.reshape(owners, width).astype(jnp.float32)


def stream(tiles_ref, held_ref, sems):
    count = tiles_ref.shape[0]
    parts = count // UNROLL
    size = UNROLL // CHUNKS

    def copy(g, i):
        at = pl.ds(g * UNROLL + i * size, size)
        return pltpu.make_async_copy(tiles_ref.at[at], held_ref.at[at], sems.at[g, i])

    for g in range(parts):
        for i in range(CHUNKS):
            copy(g, i).start()

    def ready(g):
        for i in range(CHUNKS):
            copy(g, i).wait()

    return ready


def stream_scratch(tiles):
    return [
        VMEM(tiles.shape, tiles.dtype),
        pltpu.SemaphoreType.DMA((tiles.shape[0] // UNROLL, CHUNKS)),
    ]


def pick_kernel(ids_ref, rows_ref, out_ref):
    last = rows_ref.shape[0] - 1
    turn = 48

    def step(p, carry):
        for k in range(turn):
            row = jnp.minimum(ids_ref[p * turn + k], last)
            out_ref[pl.ds(p * turn + k, 1), :] = rows_ref[pl.ds(row, 1), :]
        return carry

    lax.fori_loop(0, out_ref.shape[0] // turn, step, 0)


def pick(ids, rows):
    return pl.pallas_call(
        pick_kernel,
        name="pick",
        out_shape=jax.ShapeDtypeStruct((ids.shape[0], rows.shape[1]), jnp.float32),
        in_specs=[spec(SMEM), spec(VMEM)],
        out_specs=spec(VMEM),
        compiler_params=params(),
    )(ids, rows)


def row_kernel(slot_ref, tiles_ref, *refs):
    *pots_refs, out_ref, held_ref, sems = refs
    size = pots_refs[0].shape[0]
    ready = stream(tiles_ref, held_ref, sems)

    def potential(slot):
        if len(pots_refs) == 1:
            return pots_refs[0][pl.ds(slot, 1), :]
        side = slot // size
        near, far = (ref[pl.ds(slot - side * size, 1), :] for ref in pots_refs)
        return jnp.where(side == 0, near, far)

    def step(g, carry):
        ready(g)
        tops, sums = [], []
        for k in range(UNROLL):
            n = g * UNROLL + k
            pot = potential(slot_ref[n])
            scores = jnp.transpose(held_ref[n].astype(jnp.float32) + pot)
            top = jnp.max(scores, axis=0, keepdims=True)
            tops.append(top)
            sums.append(jnp.sum(jnp.exp(scores - top), axis=0, keepdims=True))
        block = pl.ds(pl.multiple_of(g * UNROLL, UNROLL), UNROLL)
        out_ref[block, :] = jnp.concatenate(tops, 0) + jnp.log(jnp.concatenate(sums, 0))
        return carry

    lax.fori_loop(0, tiles_ref.shape[0] // UNROLL, step, 0)


def row_pass(slot, tiles, *pots):
    return pl.pallas_call(
        row_kernel,
        name="row_pass",
        out_shape=jax.ShapeDtypeStruct(tiles.shape[:2], jnp.float32),
        in_specs=[spec(SMEM), spec(pltpu.HBM)] + [spec(VMEM)] * len(pots),
        out_specs=spec(VMEM),
        scratch_shapes=stream_scratch(tiles),
        compiler_params=params(),
    )(slot, tiles, *pots)


def col_kernel(capacity, slot_ref, tiles_ref, pots_ref, *refs):
    *ask_refs, out_ref, row_ref, held_ref, sems = refs
    ready = stream(tiles_ref, held_ref, sems)
    out_ref[...] = jnp.full(out_ref.shape, NEGATIVE, jnp.float32)
    width = tiles_ref.shape[1]
    for ask_ref in ask_refs:
        for owner in range(ask_ref.shape[0]):
            row = owner * (capacity + EXTRA) + capacity
            out_ref[row : row + 1, :] = ask_ref[owner : owner + 1, :]

    def step(g, carry):
        ready(g)
        tops, sums = [], []
        for k in range(UNROLL):
            n = g * UNROLL + k
            pot = jnp.broadcast_to(pots_ref[pl.ds(n, 1), :], (width, width))
            scores = held_ref[n].astype(jnp.float32) + jnp.transpose(pot)
            top = jnp.max(scores, axis=0, keepdims=True)
            tops.append(top)
            sums.append(jnp.sum(jnp.exp(scores - top), axis=0, keepdims=True))
        row_ref[...] = jnp.concatenate(tops, 0) + jnp.log(jnp.concatenate(sums, 0))
        for k in range(UNROLL):
            out_ref[pl.ds(slot_ref[g * UNROLL + k], 1), :] = row_ref[pl.ds(k, 1), :]
        return carry

    lax.fori_loop(0, tiles_ref.shape[0] // UNROLL, step, 0)


def col_pass(slot, tiles, pots, slots, capacity, *ask):
    width = tiles.shape[1]
    return pl.pallas_call(
        functools.partial(col_kernel, capacity),
        name="col_pass",
        out_shape=jax.ShapeDtypeStruct((slots, width), jnp.float32),
        in_specs=[spec(SMEM), spec(pltpu.HBM)] + [spec(VMEM)] * (1 + len(ask)),
        out_specs=spec(VMEM),
        scratch_shapes=[VMEM((UNROLL, width), jnp.float32)] + stream_scratch(tiles),
        compiler_params=params(),
    )(slot, tiles, pots, *ask)


def segment_kernel(capacity, ids_ref, rows_ref, out_ref, top_ref, *parts):
    sources = ids_ref.shape[0] // capacity
    stride = rows_ref.shape[0] // sources
    groups = len(parts)
    turns = sources // groups

    def walk(visit):
        for turn in range(turns):

            def step(p, carry):
                for k in range(4):
                    for g, part in enumerate(parts):
                        source = g * turns + turn
                        rank = p * 4 + k
                        visit(
                            part,
                            pl.ds(ids_ref[source * capacity + rank], 1),
                            rows_ref[pl.ds(source * stride + rank, 1), :],
                        )
                return carry

            lax.fori_loop(0, capacity // 4, step, 0)

    for part in parts:
        part[...] = jnp.full(part.shape, NEGATIVE, jnp.float32)

    def highest(part, here, row):
        part[here, :] = jnp.maximum(part[here, :], row)

    walk(highest)
    top = parts[0][...]
    for part in parts[1:]:
        top = jnp.maximum(top, part[...])
    top_ref[...] = top
    for part in parts:
        part[...] = jnp.zeros(part.shape, jnp.float32)

    def add(part, here, row):
        part[here, :] = part[here, :] + jnp.exp(row - top_ref[here, :])

    walk(add)
    total = parts[0][...]
    for part in parts[1:]:
        total = total + part[...]
    count = out_ref.shape[0]
    total = total[:count]
    some = total > 0.0
    out_ref[...] = jnp.where(
        some, top_ref[:count, :] + jnp.log(jnp.where(some, total, 1.0)), NEGATIVE
    )


def segment(ids, rows, count, capacity):
    width = rows.shape[1]
    return pl.pallas_call(
        functools.partial(segment_kernel, capacity),
        name="segment",
        out_shape=jax.ShapeDtypeStruct((count, width), jnp.float32),
        in_specs=[spec(SMEM), spec(VMEM)],
        out_specs=spec(VMEM),
        scratch_shapes=[VMEM((count + 8, width), jnp.float32)] * 9,
        compiler_params=params(),
    )(ids, rows)


def exchange(value, owners):
    shape = value.shape
    return lax.all_to_all(
        value.reshape((owners, shape[0] // owners) + shape[1:]),
        "col",
        split_axis=0,
        concat_axis=0,
        tiled=True,
    ).reshape(shape)


def log_sum(first, *others):
    top = functools.reduce(jnp.maximum, others, first)
    return top + jnp.log(sum(jnp.exp(value - top) for value in (first, *others)))


def swap(value, axis, partner):
    return lax.ppermute(value, axis, [(j, i) for i, j in enumerate(partner)])


def col_phases(count):
    def near(i, step):
        return i - i % 4 + (i + step) % 4

    def far(i, step):
        return (i + 4 * step) % count

    return [[[move(i, step) for i in range(count)] for step in (1, 3, 2)] for move in (near, far)]


def row_phases(count):
    phases = (
        ([1, 0, 3, 2, 5, 4, 7, 6],),
        ([7, 2, 1, 4, 3, 6, 5, 0], [2, 7, 4, 1, 6, 3, 0, 5], [5, 4, 7, 6, 1, 0, 3, 2]),
    )
    return [[[2 * z[i // 2] + i % 2 for i in range(count)] for z in phase] for phase in phases]


def body(kernel, tile_cols, start_pot, log_source, log_target, dustbin):
    row_tiles, local_slots, width, _ = kernel.shape
    owners = lax.axis_size("col")
    block_tiles = start_pot.shape[0] // width
    tile_count = row_tiles * local_slots
    capacity = min(tile_count // 2, 3 * tile_count // owners)
    half = block_tiles // 2
    core = lax.axis_index("row") % 2
    other_core = [i ^ 1 for i in range(lax.axis_size("row"))]

    source_rows = log_source.reshape(row_tiles, width)

    def mine(value, side):
        return lax.dynamic_slice_in_dim(value, side * half, half, 0)

    start_half = mine(start_pot.reshape(block_tiles, width), core)
    target_half = mine(log_target.reshape(block_tiles, width), core)
    dust_half = mine(dustbin.reshape(block_tiles, width), core)

    tiles = kernel.reshape(tile_count, width, width)
    owner, local, rank, ask = plan(tile_cols.reshape(tile_count), block_tiles, owners, width)
    side = local // half
    place = (side ^ core) * (owners * half) + owner * half + local - side * half
    near = exchange(jnp.tile(start_half, (owners, 1)), owners)
    far = swap(near, "row", other_core)
    for repeat in range(ITERS):
        if repeat == 0:
            row_lse = row_pass(place, tiles, near, far)
        else:
            row_lse = row_pass(
                owner * capacity + rank, tiles, exchange(pick(ids, target_now), owners)
            )
        for phase in col_phases(owners):
            row_lse = log_sum(row_lse, *[swap(row_lse, "col", partner) for partner in phase])
        source_now = source_rows - row_lse
        if repeat == 0:
            stride = capacity + EXTRA
            rows = col_pass(
                owner * stride + rank, tiles, source_now, owners * stride, capacity, ask
            )
            rows = exchange(rows, owners)
            ids = rows.reshape(owners, stride, width)[:, capacity, :capacity]
            ids = ids.astype(jnp.int32).reshape(owners * capacity)
        else:
            rows = col_pass(
                owner * capacity + rank, tiles, source_now, owners * capacity, capacity
            )
            rows = exchange(rows, owners)
        part = segment(ids, rows, block_tiles, capacity)
        col_lse = log_sum(mine(part, core), swap(mine(part, 1 - core), "row", other_core))
        for phase in row_phases(len(other_core)):
            col_lse = log_sum(col_lse, *[swap(col_lse, "row", partner) for partner in phase])
        here = target_half - log_sum(col_lse, dust_half)
        there = swap(here, "row", other_core)
        target_now = jnp.where(
            core == 0, jnp.concatenate([here, there]), jnp.concatenate([there, here])
        )
    return source_now.reshape(log_source.shape), target_now.reshape(start_pot.shape)


def solution(mesh):
    placed = (P("row", "col", None, None), P("row", "col"), P("col"), P("row"), P("col"), P("col"))
    return jax.shard_map(
        body, mesh=mesh, in_specs=placed, out_specs=(P("row"), P("col")), check_vma=False
    )
```

```python
import functools

import jax
import jax.numpy as jnp
from jax import lax
from jax.experimental import pallas as pl
from jax.experimental.pallas import tpu as pltpu
from jax.sharding import PartitionSpec as P

ITERS = 2
NEGATIVE = -1e30
VMEM = pltpu.VMEM
SMEM = pltpu.SMEM
VMEM_BYTES = 40 << 20
CHUNKS = 4
UNROLL = 64
EXTRA = 8


def spec(space):
    return pl.BlockSpec(memory_space=space)


def params():
    return pltpu.CompilerParams(vmem_limit_bytes=VMEM_BYTES)


def plan(cols, block_tiles, owners, width):
    owner = cols // block_tiles
    local = cols % block_tiles
    order = jnp.arange(cols.shape[0])
    before = (owner[:, None] == owner[None, :]) & (order[None, :] < order[:, None])
    rank = jnp.sum(before.astype(jnp.int32), axis=1)
    lane = (owner * width + rank)[:, None] == jnp.arange(owners * width)[None, :]
    ask = block_tiles + jnp.sum(jnp.where(lane, local[:, None] - block_tiles, 0), axis=0)
    return owner, local, rank, ask.reshape(owners, width).astype(jnp.float32)


def stream(tiles_ref, held_ref, sems):
    count = tiles_ref.shape[0]
    parts = count // UNROLL
    size = UNROLL // CHUNKS

    def copy(g, i):
        at = pl.ds(g * UNROLL + i * size, size)
        return pltpu.make_async_copy(tiles_ref.at[at], held_ref.at[at], sems.at[g, i])

    for g in range(parts):
        for i in range(CHUNKS):
            copy(g, i).start()

    def ready(g):
        for i in range(CHUNKS):
            copy(g, i).wait()

    return ready


def pick_kernel(ids_ref, rows_ref, out_ref):
    last = rows_ref.shape[0] - 1
    turn = 48

    def step(p, carry):
        for k in range(turn):
            row = jnp.minimum(ids_ref[p * turn + k], last)
            out_ref[pl.ds(p * turn + k, 1), :] = rows_ref[pl.ds(row, 1), :]
        return carry

    lax.fori_loop(0, out_ref.shape[0] // turn, step, 0)


def pick(ids, rows):
    return pl.pallas_call(
        pick_kernel,
        name="pick",
        out_shape=jax.ShapeDtypeStruct((ids.shape[0], rows.shape[1]), jnp.float32),
        in_specs=[spec(SMEM), spec(VMEM)],
        out_specs=spec(VMEM),
        compiler_params=params(),
    )(ids, rows)


def row_kernel(slot_ref, tiles_ref, *refs):
    *pots_refs, out_ref, held_ref, sems = refs
    size = pots_refs[0].shape[0]
    ready = stream(tiles_ref, held_ref, sems)

    def potential(slot):
        if len(pots_refs) == 1:
            return pots_refs[0][pl.ds(slot, 1), :]
        side = slot // size
        near, far = (ref[pl.ds(slot - side * size, 1), :] for ref in pots_refs)
        return jnp.where(side == 0, near, far)

    def step(g, carry):
        ready(g)
        tops, sums = [], []
        for k in range(UNROLL):
            n = g * UNROLL + k
            pot = potential(slot_ref[n])
            scores = jnp.transpose(held_ref[n].astype(jnp.float32) + pot)
            top = jnp.max(scores, axis=0, keepdims=True)
            tops.append(top)
            sums.append(jnp.sum(jnp.exp(scores - top), axis=0, keepdims=True))
        block = pl.ds(pl.multiple_of(g * UNROLL, UNROLL), UNROLL)
        out_ref[block, :] = jnp.concatenate(tops, 0) + jnp.log(jnp.concatenate(sums, 0))
        return carry

    lax.fori_loop(0, tiles_ref.shape[0] // UNROLL, step, 0)


def row_pass(slot, tiles, *pots):
    return pl.pallas_call(
        row_kernel,
        name="row_pass",
        out_shape=(
            jax.ShapeDtypeStruct(tiles.shape[:2], jnp.float32),
            VMEM(tiles.shape, tiles.dtype),
        ),
        in_specs=[spec(SMEM), spec(pltpu.HBM)] + [spec(VMEM)] * len(pots),
        out_specs=(spec(VMEM), spec(VMEM)),
        scratch_shapes=[pltpu.SemaphoreType.DMA((tiles.shape[0] // UNROLL, CHUNKS))],
        compiler_params=params(),
    )(slot, tiles, *pots)


def col_kernel(capacity, slot_ref, tiles_ref, pots_ref, *refs):
    *ask_refs, out_ref, row_ref = refs
    out_ref[...] = jnp.full(out_ref.shape, NEGATIVE, jnp.float32)
    width = tiles_ref.shape[1]
    for ask_ref in ask_refs:
        for owner in range(ask_ref.shape[0]):
            row = owner * (capacity + EXTRA) + capacity
            out_ref[row : row + 1, :] = ask_ref[owner : owner + 1, :]

    def step(g, carry):
        tops, sums = [], []
        for k in range(UNROLL):
            n = g * UNROLL + k
            pot = jnp.broadcast_to(pots_ref[pl.ds(n, 1), :], (width, width))
            scores = tiles_ref[n].astype(jnp.float32) + jnp.transpose(pot)
            top = jnp.max(scores, axis=0, keepdims=True)
            tops.append(top)
            sums.append(jnp.sum(jnp.exp(scores - top), axis=0, keepdims=True))
        row_ref[...] = jnp.concatenate(tops, 0) + jnp.log(jnp.concatenate(sums, 0))
        for k in range(UNROLL):
            out_ref[pl.ds(slot_ref[g * UNROLL + k], 1), :] = row_ref[pl.ds(k, 1), :]
        return carry

    lax.fori_loop(0, tiles_ref.shape[0] // UNROLL, step, 0)


def col_pass(slot, tiles, pots, slots, capacity, *ask):
    width = tiles.shape[1]
    return pl.pallas_call(
        functools.partial(col_kernel, capacity),
        name="col_pass",
        out_shape=jax.ShapeDtypeStruct((slots, width), jnp.float32),
        in_specs=[spec(SMEM)] + [spec(VMEM)] * (2 + len(ask)),
        out_specs=spec(VMEM),
        scratch_shapes=[VMEM((UNROLL, width), jnp.float32)],
        compiler_params=params(),
    )(slot, tiles, pots, *ask)


def segment_kernel(capacity, ids_ref, rows_ref, out_ref, top_ref, *parts):
    sources = ids_ref.shape[0] // capacity
    stride = rows_ref.shape[0] // sources
    groups = len(parts)
    turns = sources // groups

    def walk(visit):
        for turn in range(turns):

            def step(p, carry):
                for k in range(4):
                    for g, part in enumerate(parts):
                        source = g * turns + turn
                        rank = p * 4 + k
                        visit(
                            part,
                            pl.ds(ids_ref[source * capacity + rank], 1),
                            rows_ref[pl.ds(source * stride + rank, 1), :],
                        )
                return carry

            lax.fori_loop(0, capacity // 4, step, 0)

    for part in parts:
        part[...] = jnp.full(part.shape, NEGATIVE, jnp.float32)

    def highest(part, here, row):
        part[here, :] = jnp.maximum(part[here, :], row)

    walk(highest)
    top = parts[0][...]
    for part in parts[1:]:
        top = jnp.maximum(top, part[...])
    top_ref[...] = top
    for part in parts:
        part[...] = jnp.zeros(part.shape, jnp.float32)

    def add(part, here, row):
        part[here, :] = part[here, :] + jnp.exp(row - top_ref[here, :])

    walk(add)
    total = parts[0][...]
    for part in parts[1:]:
        total = total + part[...]
    count = out_ref.shape[0]
    total = total[:count]
    some = total > 0.0
    out_ref[...] = jnp.where(
        some, top_ref[:count, :] + jnp.log(jnp.where(some, total, 1.0)), NEGATIVE
    )


def segment(ids, rows, count, capacity):
    width = rows.shape[1]
    return pl.pallas_call(
        functools.partial(segment_kernel, capacity),
        name="segment",
        out_shape=jax.ShapeDtypeStruct((count, width), jnp.float32),
        in_specs=[spec(SMEM), spec(VMEM)],
        out_specs=spec(VMEM),
        scratch_shapes=[VMEM((count + 8, width), jnp.float32)] * 9,
        compiler_params=params(),
    )(ids, rows)


def exchange(value, owners):
    shape = value.shape
    return lax.all_to_all(
        value.reshape((owners, shape[0] // owners) + shape[1:]),
        "col",
        split_axis=0,
        concat_axis=0,
        tiled=True,
    ).reshape(shape)


def log_sum(first, *others):
    top = functools.reduce(jnp.maximum, others, first)
    return top + jnp.log(sum(jnp.exp(value - top) for value in (first, *others)))


def swap(value, axis, partner):
    return lax.ppermute(value, axis, [(j, i) for i, j in enumerate(partner)])


def col_phases(count):
    def near(i, step):
        return i - i % 4 + (i + step) % 4

    def far(i, step):
        return (i + 4 * step) % count

    return [[[move(i, step) for i in range(count)] for step in (2, 1, 3)] for move in (near, far)]


def row_phases(count):
    phases = (
        ([1, 0, 3, 2, 5, 4, 7, 6],),
        ([5, 4, 7, 6, 1, 0, 3, 2], [7, 2, 1, 4, 3, 6, 5, 0], [2, 7, 4, 1, 6, 3, 0, 5]),
    )
    return [[[2 * z[i // 2] + i % 2 for i in range(count)] for z in phase] for phase in phases]


def body(kernel, tile_cols, start_pot, log_source, log_target, dustbin):
    row_tiles, local_slots, width, _ = kernel.shape
    owners = lax.axis_size("col")
    block_tiles = start_pot.shape[0] // width
    tile_count = row_tiles * local_slots
    capacity = min(tile_count // 2, 3 * tile_count // owners)
    half = block_tiles // 2
    core = lax.axis_index("row") & 1
    first = core == 0
    other_core = [i ^ 1 for i in range(lax.axis_size("row"))]

    source_rows = log_source.reshape(row_tiles, width)

    def mine(value):
        return jnp.where(first, value[:half], value[half:])

    def others(value):
        return jnp.where(first, value[half:], value[:half])

    start_half = mine(start_pot.reshape(block_tiles, width))
    target_half = mine(log_target.reshape(block_tiles, width))
    dust_half = mine(dustbin.reshape(block_tiles, width))

    tiles = kernel.reshape(tile_count, width, width)
    owner, local, rank, ask = plan(tile_cols.reshape(tile_count), block_tiles, owners, width)
    side = local // half
    place = (side ^ core) * (owners * half) + owner * half + local - side * half
    near = exchange(jnp.tile(start_half, (owners, 1)), owners)
    far = swap(near, "row", other_core)
    for repeat in range(ITERS):
        if repeat == 0:
            row_lse, held = row_pass(place, tiles, near, far)
        else:
            row_lse, held = row_pass(
                owner * capacity + rank, tiles, exchange(pick(ids, target_now), owners)
            )
        for phase in col_phases(owners):
            row_lse = log_sum(row_lse, *[swap(row_lse, "col", partner) for partner in phase])
        source_now = source_rows - row_lse
        if repeat == 0:
            stride = capacity + EXTRA
            rows = col_pass(
                owner * stride + rank, held, source_now, owners * stride, capacity, ask
            )
            rows = exchange(rows, owners)
            ids = rows.reshape(owners, stride, width)[:, capacity, :capacity]
            ids = ids.astype(jnp.int32).reshape(owners * capacity)
        else:
            rows = col_pass(
                owner * capacity + rank, held, source_now, owners * capacity, capacity
            )
            rows = exchange(rows, owners)
        part = segment(ids, rows, block_tiles, capacity)
        col_lse = log_sum(mine(part), swap(others(part), "row", other_core))
        for phase in row_phases(len(other_core)):
            col_lse = log_sum(col_lse, *[swap(col_lse, "row", partner) for partner in phase])
        here = target_half - log_sum(col_lse, dust_half)
        there = swap(here, "row", other_core)
        target_now = jnp.where(
            first, jnp.concatenate([here, there]), jnp.concatenate([there, here])
        )
    return source_now.reshape(log_source.shape), target_now.reshape(start_pot.shape)


def solution(mesh):
    placed = (P("row", "col", None, None), P("row", "col"), P("col"), P("row"), P("col"), P("col"))
    return jax.shard_map(
        body, mesh=mesh, in_specs=placed, out_specs=(P("row"), P("col")), check_vma=False
    )
```

```python
import functools

import jax
import jax.numpy as jnp
from jax import lax
from jax.experimental import pallas as pl
from jax.experimental.pallas import tpu as pltpu
from jax.sharding import PartitionSpec as P

ITERS = 2
NEGATIVE = -1e30
VMEM = pltpu.VMEM
SMEM = pltpu.SMEM
VMEM_BYTES = 40 << 20
CHUNK = 16
UNROLL = 64
COL_UNROLL = 128
EXTRA = 8


def spec(space):
    return pl.BlockSpec(memory_space=space)


def params():
    return pltpu.CompilerParams(vmem_limit_bytes=VMEM_BYTES)


def plan(cols, block_tiles, owners, width):
    owner = cols // block_tiles
    local = cols % block_tiles
    order = jnp.arange(cols.shape[0])
    before = (owner[:, None] == owner[None, :]) & (order[None, :] < order[:, None])
    rank = jnp.sum(before.astype(jnp.int32), axis=1)
    lane = (owner * width + rank)[:, None] == jnp.arange(owners * width)[None, :]
    ask = block_tiles + jnp.sum(jnp.where(lane, local[:, None] - block_tiles, 0), axis=0)
    return owner, local, rank, ask.reshape(owners, width).astype(jnp.float32)


def pick_kernel(ids_ref, rows_ref, out_ref):
    turn = 48

    def step(p, carry):
        for k in range(turn):
            n = p * turn + k
            out_ref[pl.ds(n, 1), :] = rows_ref[pl.ds(ids_ref[n], 1), :]
        return carry

    lax.fori_loop(0, out_ref.shape[0] // turn, step, 0)


def pick(ids, rows):
    return pl.pallas_call(
        pick_kernel,
        name="pick",
        out_shape=jax.ShapeDtypeStruct((ids.shape[0], rows.shape[1]), jnp.float32),
        in_specs=[spec(SMEM), spec(VMEM)],
        out_specs=spec(VMEM),
        compiler_params=params(),
    )(ids, rows)


def row_kernel(slot_ref, tiles_ref, *refs):
    *pots_refs, out_ref, held_ref, sems = refs
    size = pots_refs[0].shape[0]
    chunks = sems.shape[0]

    def copy(c):
        at = pl.ds(c * CHUNK, CHUNK)
        return pltpu.make_async_copy(tiles_ref.at[at], held_ref.at[at], sems.at[c])

    for c in range(chunks):
        copy(c).start()

    def potential(slot):
        if len(pots_refs) == 1:
            return pots_refs[0][pl.ds(slot, 1), :]
        side = slot // size
        near, far = (ref[pl.ds(slot - side * size, 1), :] for ref in pots_refs)
        return jnp.where(side == 0, near, far)

    def step(count, g, carry):
        for c in range(count // CHUNK):
            copy(g * (count // CHUNK) + c).wait()
        tops, sums = [], []
        for k in range(count):
            n = g * count + k
            pot = potential(slot_ref[n])
            scores = jnp.transpose(held_ref[n].astype(jnp.float32) + pot)
            top = jnp.max(scores, axis=0, keepdims=True)
            tops.append(top)
            sums.append(jnp.sum(jnp.exp(scores - top), axis=0, keepdims=True))
        block = pl.ds(pl.multiple_of(g * count, count), count)
        out_ref[block, :] = jnp.concatenate(tops, 0) + jnp.log(jnp.concatenate(sums, 0))
        return carry

    lax.fori_loop(0, UNROLL // CHUNK, functools.partial(step, CHUNK), 0)
    lax.fori_loop(1, tiles_ref.shape[0] // UNROLL, functools.partial(step, UNROLL), 0)


def row_pass(slot, tiles, *pots):
    return pl.pallas_call(
        row_kernel,
        name="row_pass",
        out_shape=(
            jax.ShapeDtypeStruct(tiles.shape[:2], jnp.float32),
            VMEM(tiles.shape, tiles.dtype),
        ),
        in_specs=[spec(SMEM), spec(pltpu.HBM)] + [spec(VMEM)] * len(pots),
        out_specs=(spec(VMEM), spec(VMEM)),
        scratch_shapes=[pltpu.SemaphoreType.DMA((tiles.shape[0] // CHUNK,))],
        compiler_params=params(),
    )(slot, tiles, *pots)


def col_kernel(capacity, slot_ref, tiles_ref, pots_ref, *refs):
    *ask_refs, out_ref, row_ref = refs
    out_ref[...] = jnp.full(out_ref.shape, NEGATIVE, jnp.float32)
    width = tiles_ref.shape[1]
    for ask_ref in ask_refs:
        for owner in range(ask_ref.shape[0]):
            row = owner * (capacity + EXTRA) + capacity
            out_ref[row : row + 1, :] = ask_ref[owner : owner + 1, :]

    def step(g, carry):
        tops, sums = [], []
        for k in range(COL_UNROLL):
            n = g * COL_UNROLL + k
            pot = jnp.broadcast_to(pots_ref[pl.ds(n, 1), :], (width, width))
            scores = tiles_ref[n].astype(jnp.float32) + jnp.transpose(pot)
            top = jnp.max(scores, axis=0, keepdims=True)
            tops.append(top)
            sums.append(jnp.sum(jnp.exp(scores - top), axis=0, keepdims=True))
        row_ref[...] = jnp.concatenate(tops, 0) + jnp.log(jnp.concatenate(sums, 0))
        for k in range(COL_UNROLL):
            out_ref[pl.ds(slot_ref[g * COL_UNROLL + k], 1), :] = row_ref[pl.ds(k, 1), :]
        return carry

    lax.fori_loop(0, tiles_ref.shape[0] // COL_UNROLL, step, 0)


def col_pass(slot, tiles, pots, slots, capacity, *ask):
    width = tiles.shape[1]
    return pl.pallas_call(
        functools.partial(col_kernel, capacity),
        name="col_pass",
        out_shape=jax.ShapeDtypeStruct((slots, width), jnp.float32),
        in_specs=[spec(SMEM)] + [spec(VMEM)] * (2 + len(ask)),
        out_specs=spec(VMEM),
        scratch_shapes=[VMEM((COL_UNROLL, width), jnp.float32)],
        compiler_params=params(),
    )(slot, tiles, pots, *ask)


def segment_kernel(capacity, ids_ref, rows_ref, out_ref, top_ref, *parts):
    sources = ids_ref.shape[0] // capacity
    stride = rows_ref.shape[0] // sources
    groups = len(parts)
    turns = sources // groups

    def walk(visit):
        for turn in range(turns):

            def step(p, carry):
                for k in range(12):
                    for g, part in enumerate(parts):
                        source = g * turns + turn
                        rank = p * 12 + k
                        visit(
                            part,
                            pl.ds(ids_ref[source * capacity + rank], 1),
                            rows_ref[pl.ds(source * stride + rank, 1), :],
                        )
                return carry

            lax.fori_loop(0, capacity // 12, step, 0)

    for part in parts:
        part[...] = jnp.full(part.shape, NEGATIVE, jnp.float32)

    def highest(part, here, row):
        part[here, :] = jnp.maximum(part[here, :], row)

    walk(highest)
    top = parts[0][...]
    for part in parts[1:]:
        top = jnp.maximum(top, part[...])
    top_ref[...] = top
    for part in parts:
        part[...] = jnp.zeros(part.shape, jnp.float32)

    def add(part, here, row):
        part[here, :] = part[here, :] + jnp.exp(row - top_ref[here, :])

    walk(add)
    total = parts[0][...]
    for part in parts[1:]:
        total = total + part[...]
    count = out_ref.shape[0]
    total = total[:count]
    some = total > 0.0
    out_ref[...] = jnp.where(
        some, top_ref[:count, :] + jnp.log(jnp.where(some, total, 1.0)), NEGATIVE
    )


def segment(ids, rows, count, capacity):
    width = rows.shape[1]
    return pl.pallas_call(
        functools.partial(segment_kernel, capacity),
        name="segment",
        out_shape=jax.ShapeDtypeStruct((count, width), jnp.float32),
        in_specs=[spec(SMEM), spec(VMEM)],
        out_specs=spec(VMEM),
        scratch_shapes=[VMEM((count + 8, width), jnp.float32)] * 9,
        compiler_params=params(),
    )(ids, rows)


def exchange(value, owners):
    shape = value.shape
    return lax.all_to_all(
        value.reshape((owners, shape[0] // owners) + shape[1:]),
        "col",
        split_axis=0,
        concat_axis=0,
        tiled=True,
    ).reshape(shape)


def log_sum(first, *others):
    top = functools.reduce(jnp.maximum, others, first)
    return top + jnp.log(sum(jnp.exp(value - top) for value in (first, *others)))


def swap(value, axis, partner):
    return lax.ppermute(value, axis, [(j, i) for i, j in enumerate(partner)])


def col_phases(count):
    def near(i, step):
        return i - i % 4 + (i + step) % 4

    def far(i, step):
        return (i + 4 * step) % count

    return [[[move(i, step) for i in range(count)] for step in (2, 1, 3)] for move in (near, far)]


def row_phases(count):
    phases = (
        ([1, 0, 3, 2, 5, 4, 7, 6],),
        ([5, 4, 7, 6, 1, 0, 3, 2], [7, 2, 1, 4, 3, 6, 5, 0], [2, 7, 4, 1, 6, 3, 0, 5]),
    )
    return [[[2 * z[i // 2] + i % 2 for i in range(count)] for z in phase] for phase in phases]


def body(kernel, tile_cols, start_pot, log_source, log_target, dustbin):
    row_tiles, local_slots, width, _ = kernel.shape
    owners = lax.axis_size("col")
    block_tiles = start_pot.shape[0] // width
    tile_count = row_tiles * local_slots
    capacity = min(tile_count // 2, 3 * tile_count // owners)
    half = block_tiles // 2
    core = lax.axis_index("row") & 1
    first = core == 0
    other_core = [i ^ 1 for i in range(lax.axis_size("row"))]

    source_rows = log_source.reshape(row_tiles, width)

    def mine(value):
        return jnp.where(first, value[:half], value[half:])

    def others(value):
        return jnp.where(first, value[half:], value[:half])

    start_half = lax.dynamic_slice_in_dim(
        start_pot.reshape(block_tiles, width), core * half, half, 0
    )
    target_half = mine(log_target.reshape(block_tiles, width))
    dust_half = mine(dustbin.reshape(block_tiles, width))

    tiles = kernel.reshape(tile_count, width, width)
    owner, local, rank, ask = plan(tile_cols.reshape(tile_count), block_tiles, owners, width)
    side = local // half
    place = (side ^ core) * (owners * half) + owner * half + local - side * half
    near = exchange(jnp.tile(start_half, (owners, 1)), owners)
    far = swap(near, "row", other_core)
    for repeat in range(ITERS):
        if repeat == 0:
            row_lse, held = row_pass(place, tiles, near, far)
        else:
            row_lse, held = row_pass(
                owner * capacity + rank, tiles, exchange(pick(picked, target_now), owners)
            )
        for phase in col_phases(owners):
            row_lse = log_sum(row_lse, *[swap(row_lse, "col", partner) for partner in phase])
        source_now = source_rows - row_lse
        if repeat == 0:
            stride = capacity + EXTRA
            rows = col_pass(
                owner * stride + rank, held, source_now, owners * stride, capacity, ask
            )
            rows = exchange(rows, owners)
            ids = rows.reshape(owners, stride, width)[:, capacity, :capacity]
            ids = ids.astype(jnp.int32).reshape(owners * capacity)
            picked = jnp.minimum(ids, block_tiles - 1)
        else:
            rows = col_pass(
                owner * capacity + rank, held, source_now, owners * capacity, capacity
            )
            rows = exchange(rows, owners)
        part = segment(ids, rows, block_tiles, capacity)
        col_lse = log_sum(mine(part), swap(others(part), "row", other_core))
        for phase in row_phases(len(other_core)):
            col_lse = log_sum(col_lse, *[swap(col_lse, "row", partner) for partner in phase])
        here = target_half - log_sum(col_lse, dust_half)
        there = swap(here, "row", other_core)
        target_now = jnp.where(
            first, jnp.concatenate([here, there]), jnp.concatenate([there, here])
        )
    return source_now.reshape(log_source.shape), target_now.reshape(start_pot.shape)


def solution(mesh):
    placed = (P("row", "col", None, None), P("row", "col"), P("col"), P("row"), P("col"), P("col"))
    return jax.shard_map(
        body, mesh=mesh, in_specs=placed, out_specs=(P("row"), P("col")), check_vma=False
    )
```

```python
import functools

import jax
import jax.numpy as jnp
from jax import lax
from jax.experimental import pallas as pl
from jax.experimental.pallas import tpu as pltpu
from jax.sharding import PartitionSpec as P

ITERS = 2
NEGATIVE = -1e30
VMEM = pltpu.VMEM
SMEM = pltpu.SMEM
VMEM_BYTES = 40 << 20
CHUNK = 16
UNROLL = 64
COL_UNROLL = 128
EXTRA = 8


def spec(space):
    return pl.BlockSpec(memory_space=space)


def params():
    return pltpu.CompilerParams(vmem_limit_bytes=VMEM_BYTES)


def plan(cols, block_tiles, owners, width):
    owner = cols // block_tiles
    local = cols % block_tiles
    order = jnp.arange(cols.shape[0])
    before = (owner[:, None] == owner[None, :]) & (order[None, :] < order[:, None])
    rank = jnp.sum(before.astype(jnp.int32), axis=1)
    lane = (owner * width + rank)[:, None] == jnp.arange(owners * width)[None, :]
    ask = block_tiles + jnp.sum(jnp.where(lane, local[:, None] - block_tiles, 0), axis=0)
    return owner, local, rank, ask.reshape(owners, width).astype(jnp.float32)


def pick_kernel(ids_ref, rows_ref, out_ref):
    turn = 48

    def step(p, carry):
        for k in range(turn):
            n = p * turn + k
            out_ref[pl.ds(n, 1), :] = rows_ref[pl.ds(ids_ref[n], 1), :]
        return carry

    lax.fori_loop(0, out_ref.shape[0] // turn, step, 0)


def pick(ids, rows):
    return pl.pallas_call(
        pick_kernel,
        name="pick",
        out_shape=jax.ShapeDtypeStruct((ids.shape[0], rows.shape[1]), jnp.float32),
        in_specs=[spec(SMEM), spec(VMEM)],
        out_specs=spec(VMEM),
        compiler_params=params(),
    )(ids, rows)


def row_kernel(slot_ref, tiles_ref, *refs):
    *pots_refs, out_ref, held_ref, sems = refs
    size = pots_refs[0].shape[0]
    chunks = sems.shape[0]

    def copy(c):
        at = pl.ds(c * CHUNK, CHUNK)
        return pltpu.make_async_copy(tiles_ref.at[at], held_ref.at[at], sems.at[c])

    for c in range(chunks):
        copy(c).start()

    def potential(slot):
        if len(pots_refs) == 1:
            return pots_refs[0][pl.ds(slot, 1), :]
        side = slot // size
        near, far = (ref[pl.ds(slot - side * size, 1), :] for ref in pots_refs)
        return jnp.where(side == 0, near, far)

    def step(count, g, carry):
        for c in range(count // CHUNK):
            copy(g * (count // CHUNK) + c).wait()
        tops, sums = [], []
        for k in range(count):
            n = g * count + k
            pot = potential(slot_ref[n])
            scores = jnp.transpose(held_ref[n].astype(jnp.float32) + pot)
            top = jnp.max(scores, axis=0, keepdims=True)
            tops.append(top)
            sums.append(jnp.sum(jnp.exp(scores - top), axis=0, keepdims=True))
        block = pl.ds(pl.multiple_of(g * count, count), count)
        out_ref[block, :] = jnp.concatenate(tops, 0) + jnp.log(jnp.concatenate(sums, 0))
        return carry

    lax.fori_loop(0, UNROLL // CHUNK, functools.partial(step, CHUNK), 0)
    lax.fori_loop(1, tiles_ref.shape[0] // UNROLL, functools.partial(step, UNROLL), 0)


def row_pass(slot, tiles, *pots):
    return pl.pallas_call(
        row_kernel,
        name="row_pass",
        out_shape=(
            jax.ShapeDtypeStruct(tiles.shape[:2], jnp.float32),
            VMEM(tiles.shape, tiles.dtype),
        ),
        in_specs=[spec(SMEM), spec(pltpu.HBM)] + [spec(VMEM)] * len(pots),
        out_specs=(spec(VMEM), spec(VMEM)),
        scratch_shapes=[pltpu.SemaphoreType.DMA((tiles.shape[0] // CHUNK,))],
        compiler_params=params(),
    )(slot, tiles, *pots)


def col_kernel(capacity, slot_ref, tiles_ref, pots_ref, *refs):
    *ask_refs, out_ref, row_ref = refs
    out_ref[...] = jnp.full(out_ref.shape, NEGATIVE, jnp.float32)
    width = tiles_ref.shape[1]
    for ask_ref in ask_refs:
        for owner in range(ask_ref.shape[0]):
            row = owner * (capacity + EXTRA) + capacity
            out_ref[row : row + 1, :] = ask_ref[owner : owner + 1, :]

    def step(g, carry):
        tops, sums = [], []
        for k in range(COL_UNROLL):
            n = g * COL_UNROLL + k
            pot = jnp.broadcast_to(pots_ref[pl.ds(n, 1), :], (width, width))
            scores = tiles_ref[n].astype(jnp.float32) + jnp.transpose(pot)
            top = jnp.max(scores, axis=0, keepdims=True)
            tops.append(top)
            sums.append(jnp.sum(jnp.exp(scores - top), axis=0, keepdims=True))
        row_ref[...] = jnp.concatenate(tops, 0) + jnp.log(jnp.concatenate(sums, 0))
        for k in range(COL_UNROLL):
            out_ref[pl.ds(slot_ref[g * COL_UNROLL + k], 1), :] = row_ref[pl.ds(k, 1), :]
        return carry

    lax.fori_loop(0, tiles_ref.shape[0] // COL_UNROLL, step, 0)


def col_pass(slot, tiles, pots, slots, capacity, *ask):
    width = tiles.shape[1]
    return pl.pallas_call(
        functools.partial(col_kernel, capacity),
        name="col_pass",
        out_shape=jax.ShapeDtypeStruct((slots, width), jnp.float32),
        in_specs=[spec(SMEM)] + [spec(VMEM)] * (2 + len(ask)),
        out_specs=spec(VMEM),
        scratch_shapes=[VMEM((COL_UNROLL, width), jnp.float32)],
        compiler_params=params(),
    )(slot, tiles, pots, *ask)


def segment_kernel(capacity, ids_ref, rows_ref, out_ref, top_ref, *parts):
    sources = ids_ref.shape[0] // capacity
    stride = rows_ref.shape[0] // sources
    groups = len(parts)
    turns = sources // groups

    def walk(visit):
        for turn in range(turns):

            def step(p, carry):
                for k in range(12):
                    for g, part in enumerate(parts):
                        source = g * turns + turn
                        rank = p * 12 + k
                        visit(
                            part,
                            pl.ds(ids_ref[source * capacity + rank], 1),
                            rows_ref[pl.ds(source * stride + rank, 1), :],
                        )
                return carry

            lax.fori_loop(0, capacity // 12, step, 0)

    for part in parts:
        part[...] = jnp.full(part.shape, NEGATIVE, jnp.float32)

    def highest(part, here, row):
        part[here, :] = jnp.maximum(part[here, :], row)

    walk(highest)
    top = parts[0][...]
    for part in parts[1:]:
        top = jnp.maximum(top, part[...])
    top_ref[...] = top
    for part in parts:
        part[...] = jnp.zeros(part.shape, jnp.float32)

    def add(part, here, row):
        part[here, :] = part[here, :] + jnp.exp(row - top_ref[here, :])

    walk(add)
    total = parts[0][...]
    for part in parts[1:]:
        total = total + part[...]
    count = out_ref.shape[0]
    total = total[:count]
    some = total > 0.0
    out_ref[...] = jnp.where(
        some, top_ref[:count, :] + jnp.log(jnp.where(some, total, 1.0)), NEGATIVE
    )


def segment(ids, rows, count, capacity):
    width = rows.shape[1]
    return pl.pallas_call(
        functools.partial(segment_kernel, capacity),
        name="segment",
        out_shape=jax.ShapeDtypeStruct((count, width), jnp.float32),
        in_specs=[spec(SMEM), spec(VMEM)],
        out_specs=spec(VMEM),
        scratch_shapes=[VMEM((count + 8, width), jnp.float32)] * 9,
        compiler_params=params(),
    )(ids, rows)


def exchange(value, owners):
    shape = value.shape
    return lax.all_to_all(
        value.reshape((owners, shape[0] // owners) + shape[1:]),
        "col",
        split_axis=0,
        concat_axis=0,
        tiled=True,
    ).reshape(shape)


def log_sum(first, *others):
    top = functools.reduce(jnp.maximum, others, first)
    return top + jnp.log(sum(jnp.exp(value - top) for value in (first, *others)))


def swap(value, axis, partner):
    return lax.ppermute(value, axis, [(j, i) for i, j in enumerate(partner)])


def col_phases(count):
    def near(i, step):
        return i - i % 4 + (i + step) % 4

    def far(i, step):
        return (i + 4 * step) % count

    return [[[move(i, step) for i in range(count)] for step in (2, 1, 3)] for move in (near, far)]


def row_phases(count):
    phases = (
        ([1, 0, 3, 2, 5, 4, 7, 6],),
        ([5, 4, 7, 6, 1, 0, 3, 2], [7, 2, 1, 4, 3, 6, 5, 0], [2, 7, 4, 1, 6, 3, 0, 5]),
    )
    return [[[2 * z[i // 2] + i % 2 for i in range(count)] for z in phase] for phase in phases]


def body(kernel, tile_cols, start_pot, log_source, log_target, dustbin):
    row_tiles, local_slots, width, _ = kernel.shape
    owners = lax.axis_size("col")
    block_tiles = start_pot.shape[0] // width
    tile_count = row_tiles * local_slots
    capacity = min(tile_count // 2, 3 * tile_count // owners)
    half = block_tiles // 2
    core = lax.axis_index("row") & 1
    other_core = [i ^ 1 for i in range(lax.axis_size("row"))]

    source_rows = log_source.reshape(row_tiles, width)

    def mine(value):
        return jnp.where(first, value[:half], value[half:])

    def others(value):
        return jnp.where(first, value[half:], value[:half])

    start_half = lax.dynamic_slice_in_dim(
        start_pot.reshape(block_tiles, width), core * half, half, 0
    )
    tiles = kernel.reshape(tile_count, width, width)
    owner, local, rank, ask = plan(tile_cols.reshape(tile_count), block_tiles, owners, width)
    side = local // half
    place = (side ^ core) * (owners * half) + owner * half + local - side * half
    near = exchange(jnp.tile(start_half, (owners, 1)), owners)
    far = swap(near, "row", other_core)
    place, first = lax.optimization_barrier((place, core == 0))
    target_half = mine(log_target.reshape(block_tiles, width))
    dust_half = mine(dustbin.reshape(block_tiles, width))
    for repeat in range(ITERS):
        if repeat == 0:
            row_lse, held = row_pass(place, tiles, near, far)
        else:
            row_lse, held = row_pass(
                owner * capacity + rank, tiles, exchange(pick(picked, target_now), owners)
            )
        for phase in col_phases(owners):
            row_lse = log_sum(row_lse, *[swap(row_lse, "col", partner) for partner in phase])
        source_now = source_rows - row_lse
        if repeat == 0:
            stride = capacity + EXTRA
            rows = col_pass(
                owner * stride + rank, held, source_now, owners * stride, capacity, ask
            )
            rows = exchange(rows, owners)
            ids = rows.reshape(owners, stride, width)[:, capacity, :capacity]
            ids = ids.astype(jnp.int32).reshape(owners * capacity)
            picked = jnp.minimum(ids, block_tiles - 1)
        else:
            rows = col_pass(
                owner * capacity + rank, held, source_now, owners * capacity, capacity
            )
            rows = exchange(rows, owners)
        part = segment(ids, rows, block_tiles, capacity)
        col_lse = log_sum(mine(part), swap(others(part), "row", other_core))
        for phase in row_phases(len(other_core)):
            col_lse = log_sum(col_lse, *[swap(col_lse, "row", partner) for partner in phase])
        here = target_half - log_sum(col_lse, dust_half)
        there = swap(here, "row", other_core)
        target_now = jnp.where(
            first, jnp.concatenate([here, there]), jnp.concatenate([there, here])
        )
    return source_now.reshape(log_source.shape), target_now.reshape(start_pot.shape)


def solution(mesh):
    placed = (P("row", "col", None, None), P("row", "col"), P("col"), P("row"), P("col"), P("col"))
    return jax.shard_map(
        body, mesh=mesh, in_specs=placed, out_specs=(P("row"), P("col")), check_vma=False
    )
```
